256 devices in a mesh: label: 8 (over y_hi, x), dp: 32 (over z, y_lo, core).
Axes of the slice: x: 4, y: 4 (y_hi: 2, y_lo: 2; y = y_hi * 2 + y_lo), z: 8, core: 2. Of those that a mesh axis runs over, the one named last changes fastest.
Arguments:
- queries: bfloat16 [12288, 768], P(('label', 'dp')), may hold values from -6 to 6
- positives: int32 [12288, 8], P(('label', 'dp')), may hold values from 0 to 65535
- row_weight: float32 [12288], P(('label', 'dp')), may hold values from 0.02 to 0.2
- label_weight: bfloat16 [65536, 768], P('label'), may hold values from -0.21875 to 0.21875
Outputs:
- query_grad: float32 [12288, 768], P(('label', 'dp'))
- weight_grad: float32 [65536, 768], P(('label', 'dp'))
The draws below stay inside these ranges and needn't reach their ends.
All inputs are finite; a program needn't handle non-finite values.
Results may differ from the reference program's by a relative error of at most 0.013.
Values may be sent and summed in bfloat16 or wider, within the bound.
A program may use at most 128 MiB of HBM per device.

```python
import math
import jax
import jax.numpy as jnp
from jax import lax

D = 768
LAB_DEV = 8192
POS = 8
LABELS = 65536
ROWS = 12288
N_LABEL = 8


def plant(entries, rng, smallest, largest):
    longest = entries.shape.index(max(entries.shape))
    spots = []
    for shift in (0, 1):
        where = [jax.random.randint(jax.random.fold_in(rng, axis), (), 0, length) for axis, length in enumerate(entries.shape)]
        where[longest] = (where[longest] + shift) % entries.shape[longest]
        spots.append(tuple(where))
    return entries.at[spots[0]].set(smallest).at[spots[1]].set(largest)


def block_levels(key, dims, cuts, smallest, largest):
    gain = 1.0
    for dim, blocks in cuts:
        steps = jax.random.uniform(jax.random.fold_in(jax.random.fold_in(key, 6), dim), (blocks,), jnp.float32, smallest / len(cuts), largest / len(cuts))
        gain = gain * jnp.repeat(jnp.exp(steps), dims[dim] // blocks).reshape((-1,) + (1,) * (len(dims) - 1 - dim))
    return gain


def normal_values(rng, shape, spread, reach, pieces=(), held_as=jnp.bfloat16):
    loudness = block_levels(rng, shape, pieces, -0.22, 0.18) if pieces else 1.0
    entries = jax.random.normal(rng, shape, jnp.float32) * spread * loudness
    return jnp.minimum(jnp.maximum(entries, -reach), reach).astype(held_as)


def setup_inputs(seed: int = 0) -> dict:
    streams_of = jax.random.split(jax.random.key(seed), 5)
    queries = normal_values(streams_of[0], (ROWS, D), 1.0, 6.0, ((0, 256),))
    positives = plant(jax.random.randint(streams_of[1], (ROWS, POS), 0, LABELS), jax.random.fold_in(streams_of[1], 1), 0, LABELS - 1).astype(jnp.int32)
    row_weight = jnp.clip(jnp.exp(math.log(0.2) - 2.3025851 * jax.random.uniform(streams_of[2], (ROWS,), jnp.float32) ** block_levels(streams_of[2], (ROWS,), ((0, 256),), -0.2, 0.2)), 0.02, 0.2)
    label_weight = normal_values(streams_of[3], (LABELS, D), D ** -0.5, 0.21875, ((0, 8),))
    return {"queries": queries, "positives": positives, "row_weight": row_weight, "label_weight": label_weight}


def reference(queries, positives, row_weight, label_weight):
    def block(j):
        weights = lax.dynamic_slice_in_dim(label_weight, j * LAB_DEV, LAB_DEV, 0)
        label_ids = j * LAB_DEV + lax.iota(jnp.int32, LAB_DEV)
        logits = lax.dot_general(queries, weights, (((1,), (1,)), ((), ())), preferred_element_type=jnp.float32)
        targets = jnp.zeros((ROWS, LAB_DEV), jnp.float32)
        for slot in range(POS):
            match = (positives[:, slot][:, None] == label_ids[None, :]).astype(jnp.float32)
            targets = jnp.maximum(targets, match)
        grads = (row_weight[:, None] * (jax.nn.sigmoid(logits) - targets)).astype(jnp.bfloat16)
        query_part = jnp.dot(grads, weights, preferred_element_type=jnp.float32)
        weight_part = lax.dot_general(grads, queries, (((0,), (0,)), ((), ())), preferred_element_type=jnp.float32)
        return query_part, weight_part

    query_parts, weight_parts = lax.map(block, jnp.arange(N_LABEL, dtype=jnp.int32))
    return jnp.sum(query_parts, axis=0), weight_parts.reshape(LABELS, D)
```

```python
import functools

import jax
import jax.numpy as jnp
from jax import lax
from jax.experimental import pallas as pl
from jax.experimental.pallas import tpu as pltpu
from jax.sharding import PartitionSpec as P

MESH = pl.DeviceIdType.MESH
BF16, F32 = jnp.bfloat16, jnp.float32

ROWS, D, POS = 48, 768, 8
WIDE = D + 128
PLANE = 32 * ROWS
LAB, NZ = 256, 8
HALF = LAB // 2
CUT = 512
COLS = D // 2


def pack_rows(positives, weight_row):
    lane = lax.broadcasted_iota(jnp.int32, (ROWS, 128), 1)
    eye = lax.broadcasted_iota(jnp.int32, (ROWS, ROWS), 0) == lax.broadcasted_iota(
        jnp.int32, (ROWS, ROWS), 1
    )
    weight = jnp.sum(jnp.where(eye, weight_row, 0.0), axis=1, keepdims=True)
    first = weight.astype(BF16).astype(F32)
    rest = weight - first
    second = rest.astype(BF16).astype(F32)
    third = rest - second
    out = jnp.zeros((ROWS, 128), F32)
    for k, part in enumerate((first, second, third)):
        out = jnp.where(lane == 2 * POS + k, part, out)
    for s in range(POS):
        column = positives[:, s : s + 1]
        out = jnp.where(lane == s, (column >> 8).astype(F32), out)
        out = jnp.where(lane == POS + s, (column & 255).astype(F32), out)
    return out.astype(BF16)


def unpack_matrix():
    row = lax.broadcasted_iota(jnp.int32, (16, 128), 0)
    lane = lax.broadcasted_iota(jnp.int32, (16, 128), 1)
    out = jnp.where((lane == row) & (row < POS), 256.0, 0.0)
    out = jnp.where((lane == row + POS) & (row < POS), 1.0, out)
    out = jnp.where((row == POS) & (lane >= 2 * POS) & (lane < 2 * POS + 3), 0.5, out)
    return out.astype(BF16)


def kernel(
    queries,
    positives,
    weight,
    labels,
    query_grad,
    weight_grad,
    q,
    w,
    qg,
    wg,
    g,
    bits,
    half_weight,
    zs,
    zr,
    sib_s,
    sib_r,
    one_s,
    one_r,
    two_s,
    two_r,
    w_sem,
    send_sem,
    recv_sem,
):
    l, d = lax.axis_index("label"), lax.axis_index("dp")
    x, y, z, c = l % 4, (l // 4) * 2 + (d // 2) % 2, d // 4, d % 2
    yc = d % 4
    other = 1 - c
    a, b = jnp.where(c == 0, x, y), jnp.where(c == 0, y, x)

    def device(x, y, z, c):
        return ((y // 2) * 4 + x, z * 4 + (y % 2) * 2 + c)

    def in_plane(a, b):
        return device(jnp.where(c == 0, a, b), jnp.where(c == 0, b, a), z, c)

    def turn(v, k):
        return (v + k + 4) % 4

    a_up, a_down = in_plane(turn(a, 1), b), in_plane(turn(a, -1), b)
    b_up, b_down = in_plane(a, turn(b, 1)), in_plane(a, turn(b, -1))
    z_up, z_down = device(x, y, (z + 1) % 8, c), device(x, y, (z + 7) % 8, c)
    sibling = device(x, y, z, other)

    loads = []
    for k in range(NZ):
        start = pl.multiple_of((k * 4 + yc) * LAB, LAB)
        load = pltpu.make_async_copy(labels.at[pl.ds(start, LAB)], w.at[k], w_sem.at[k])
        load.start()
        loads.append(load)

    barrier = pltpu.get_barrier_semaphore()
    for partner in (a_up, a_down, b_up, b_down, z_up, z_down, sibling):
        pl.semaphore_signal(barrier, inc=1, device_id=partner, device_id_type=MESH)

    def rows_of(cc, bb, aa, count=1):
        return pl.ds(pl.multiple_of(((cc * 4 + bb) * 4 + aa) * ROWS, ROWS), count * ROWS)

    own = rows_of(c, b, a)
    q[own, :D] = queries[...]
    q[own, D:] = pack_rows(positives[...], weight[...])
    pl.semaphore_wait(barrier, 7)

    copies = []

    def send(src, dst, to):
        i = len(copies)
        copy = pltpu.make_async_remote_copy(
            src_ref=src,
            dst_ref=dst,
            send_sem=send_sem.at[i],
            recv_sem=recv_sem.at[i],
            device_id=to,
            device_id_type=MESH,
        )
        copy.start()
        copies.append(copy)
        return copy

    def spread(rows, to, lo=0, hi=WIDE):
        place = q.at[rows, pl.ds(lo, hi - lo)]
        return send(place, place, to)

    order = (0, -1, 1, 2)
    spot = [turn(a, k) for k in order]

    def pieces(bb):
        return [rows_of(c, bb, aa) for aa in spot]

    here, below, above, across = (pieces(turn(b, k)) for k in order)
    up1 = spread(here[0], a_up)
    down1 = spread(here[0], a_down)
    b_up1, b_down1, b_up2, b_down2 = [], [], [], []
    b_up1.append(spread(here[0], b_up))
    b_down1.append(spread(here[0], b_down))
    up1.wait_recv()
    up2 = spread(here[1], a_up, 0, CUT)
    b_up1.append(spread(here[1], b_up))
    b_down1.append(spread(here[1], b_down))
    down1.wait_recv()
    down2 = spread(here[2], a_down, CUT, WIDE)
    b_up1.append(spread(here[2], b_up))
    b_down1.append(spread(here[2], b_down))
    to_sibling = [spread(here[k], sibling) for k in range(3)]
    up2.wait_recv()
    down2.wait_recv()
    b_up1.append(spread(here[3], b_up))
    b_down1.append(spread(here[3], b_down))
    to_sibling.append(spread(here[3], sibling))
    for k in range(4):
        b_up1[k].wait_recv()
        b_up2.append(spread(below[k], b_up, 0, CUT))
        to_sibling.append(spread(below[k], sibling))
        b_down1[k].wait_recv()
        b_down2.append(spread(above[k], b_down, CUT, WIDE))
        to_sibling.append(spread(above[k], sibling))
    qg[...] = jnp.zeros_like(qg)
    for k in range(4):
        b_up2[k].wait_recv()
        b_down2[k].wait_recv()
        to_sibling.append(spread(across[k], sibling))
    for copy in to_sibling:
        copy.wait_recv()
    for load in loads:
        load.wait()

    unpacked = lax.dot_general(
        unpack_matrix(), q[:, D:], (((1,), (1,)), ((), ())), preferred_element_type=F32
    )
    half_weight[...] = jnp.broadcast_to(unpacked[POS : POS + 1], (8, PLANE))
    label = unpacked[:POS].astype(jnp.int32) - l * (4 * NZ * LAB)
    mine = (label >= 0) & (label < 4 * NZ * LAB) & ((label >> 8) % 4 == yc)
    word = jnp.where(mine, (label >> 10) * 8 + (label & 7), -1)
    bit = lax.shift_left(jnp.int32(1), (label >> 3) & 31)
    sub = lax.broadcasted_iota(jnp.int32, (8, PLANE), 0)
    for k in range(NZ):
        held = jnp.zeros((8, PLANE), jnp.int32)
        for s in range(POS):
            held = held | jnp.where(word[s : s + 1] == k * 8 + sub, bit[s : s + 1], 0)
        bits[k] = held

    sent_up, sent_down = [], []

    def pass_on(m, block, first, second):
        for way, (part, half) in enumerate((first, second)):
            rows = pl.ds(half * HALF, HALF)
            total = wg[part, rows, :]
            if m >= 2:
                (sent_up, sent_down)[way][m - 2].wait_recv()
                total = total + zr[way, m - 2].astype(F32)
            zs[way, m] = total.astype(BF16)
            copy = send(zs.at[way, m], zr.at[way, m], (z_up, z_down)[way])
            (sent_up, sent_down)[way].append(copy)

    def compute(j):
        size = 4 - (j + 1) // 2
        plane = (z + jnp.where(j % 2 == 1, size, 8 - size)) % 8
        block = w[plane]
        logits = lax.dot_general(
            block, q[:, :D], (((1,), (1,)), ((), ())), preferred_element_type=F32
        )
        held, scale = bits[plane], half_weight[...]
        parts = []
        for k in range(LAB // 8):
            mask = jnp.int32(1 << k if k < 31 else -(1 << 31))
            target = jnp.where((held & mask) != 0, -1.0, 1.0)
            parts.append(scale * (jnp.tanh(0.5 * logits[8 * k : 8 * k + 8]) + target))
        g[...] = jnp.concatenate(parts, axis=0).astype(BF16)
        qg[...] += lax.dot_general(
            g[...], block, (((0,), (0,)), ((), ())), preferred_element_type=F32
        )
        wg[j] = jnp.dot(g[...], q[:, :D], preferred_element_type=F32)

    def stretch(lo, hi):
        @pl.loop(lo, hi)
        def _(j):
            compute(j)

    stretch(0, 1)
    pass_on(0, 0, (0, 0), (0, 1))
    stretch(1, 3)
    pass_on(1, 1, (1, 1), (2, 0))
    stretch(3, 4)
    pass_on(2, 1, (1, 0), (2, 1))
    stretch(4, 6)
    pass_on(3, 3, (3, 1), (4, 0))
    stretch(6, 8)
    pass_on(4, 3, (3, 0), (4, 1))

    passed = []
    for i, k in enumerate((2, 1, -1, 0)):
        sib_s[i] = qg[rows_of(other, turn(a, k), 0, 4), :].astype(BF16)
        passed.append(send(sib_s.at[i], sib_r.at[i], sibling))
    groups = [rows_of(c, turn(b, k), 0, 4) for k in (2, 1, -1, 0)]
    left, right = slice(0, COLS), slice(COLS, D)

    def ring(group, outgoing, incoming, up, down, prepare, between):
        def start(m, way, block, cols):
            outgoing[way, m] = qg[group[block], cols].astype(outgoing.dtype)
            return send(outgoing.at[way, m], incoming.at[way, m], (up, down)[way])

        def add(copy, m, way, block, cols):
            copy.wait_recv()
            qg[group[block], cols] += incoming[way, m].astype(F32)

        prepare(0)
        up0, down0 = start(0, 0, 0, left), start(0, 1, 0, right)
        prepare(1)
        up1 = start(1, 0, 1, right)
        prepare(2)
        down1 = start(1, 1, 2, left)
        prepare(3)
        between()
        add(up0, 0, 0, 1, left)
        up2 = start(2, 0, 1, left)
        add(down0, 0, 1, 2, right)
        down2 = start(2, 1, 2, right)
        add(up1, 1, 0, 3, right)
        add(down1, 1, 1, 3, left)
        add(up2, 2, 0, 3, left)
        add(down2, 2, 1, 3, right)

    def from_sibling(i):
        passed[i].wait_recv()
        qg[groups[i], :] += sib_r[i].astype(F32)

    ring(
        groups,
        one_s,
        one_r,
        b_up,
        b_down,
        from_sibling,
        lambda: pass_on(5, 5, (5, 1), (6, 0)),
    )
    blocks = [rows_of(c, b, turn(a, k)) for k in (2, 1, -1, 0)]
    ring(
        blocks,
        two_s,
        two_r,
        a_up,
        a_down,
        lambda i: None,
        lambda: pass_on(6, 5, (5, 0), (6, 1)),
    )
    query_grad[...] = qg[own, :]

    low, high = pl.ds(0, HALF), pl.ds(HALF, HALF)
    for m, (up_rows, down_rows) in ((5, (high, low)), (6, (low, high))):
        sent_up[m].wait_recv()
        wg[7, up_rows, :] += zr[0, m].astype(F32)
        sent_down[m].wait_recv()
        wg[7, down_rows, :] += zr[1, m].astype(F32)
    weight_grad[...] = wg[7]

    for copy in copies:
        copy.wait_send()


COPIES = 2 + 8 + 2 + 16 + 8 + 14 + 4 + 6 + 6


def on_device(queries, positives, row_weight, label_weight):
    vmem = pl.BlockSpec(memory_space=pltpu.VMEM)
    return pl.pallas_call(
        kernel,
        out_shape=(
            jax.ShapeDtypeStruct((ROWS, D), F32),
            jax.ShapeDtypeStruct((LAB, D), F32),
        ),
        in_specs=[vmem, vmem, vmem, pl.BlockSpec(memory_space=pl.ANY)],
        out_specs=(vmem, vmem),
        scratch_shapes=[
            pltpu.VMEM((PLANE, WIDE), BF16),
            pltpu.VMEM((NZ, LAB, D), BF16),
            pltpu.VMEM((PLANE, D), F32),
            pltpu.VMEM((NZ, LAB, D), F32),
            pltpu.VMEM((LAB, PLANE), BF16),
            pltpu.VMEM((NZ, 8, PLANE), jnp.int32),
            pltpu.VMEM((8, PLANE), F32),
            pltpu.VMEM((2, 7, HALF, D), BF16),
            pltpu.VMEM((2, 7, HALF, D), BF16),
            pltpu.VMEM((4, 4 * ROWS, D), BF16),
            pltpu.VMEM((4, 4 * ROWS, D), BF16),
            pltpu.VMEM((2, 3, 4 * ROWS, COLS), BF16),
            pltpu.VMEM((2, 3, 4 * ROWS, COLS), BF16),
            pltpu.VMEM((2, 3, ROWS, COLS), F32),
            pltpu.VMEM((2, 3, ROWS, COLS), F32),
            pltpu.SemaphoreType.DMA((NZ,)),
            pltpu.SemaphoreType.DMA((COPIES,)),
            pltpu.SemaphoreType.DMA((COPIES,)),
        ],
        compiler_params=pltpu.CompilerParams(
            collective_id=0, has_side_effects=True, vmem_limit_bytes=56 * 2**20
        ),
        cost_estimate=pl.CostEstimate(
            flops=6 * PLANE * NZ * LAB * D, bytes_accessed=NZ * LAB * D * 2, transcendentals=0
        ),
    )(queries, positives, row_weight[None, :], label_weight)


def solution(mesh):
    placed = (
        P(("label", "dp"), None),
        P(("label", "dp"), None),
        P(("label", "dp")),
        P("label", None),
    )
    return jax.shard_map(
        on_device,
        mesh=mesh,
        in_specs=placed,
        out_specs=(P(("label", "dp"), None), P(("label", "dp"), None)),
        check_vma=False,
    )
```

```python
import functools

import jax
import jax.numpy as jnp
from jax import lax
from jax.experimental import pallas as pl
from jax.experimental.pallas import tpu as pltpu
from jax.sharding import PartitionSpec as P

MESH = pl.DeviceIdType.MESH
BF16, F32 = jnp.bfloat16, jnp.float32

ROWS, D, POS = 48, 768, 8
PLANE = 32 * ROWS
LAB, NZ = 256, 8
HALF = LAB // 2
CHUNK = 8 * ROWS
RING = (2, 1, -1, 0)
BACK = (0, 2, 1, 3)
HOME = 3
AWAY = (2, -2, 1, -1, 0, 3, -3, 4)


def pack_rows(positives, weight):
    high, low = positives >> 8, positives & 255
    first = weight.astype(BF16).astype(F32)
    rest = weight - first
    second = rest.astype(BF16).astype(F32)
    third = rest - second
    row = lax.broadcasted_iota(jnp.int32, (16, ROWS), 0)
    weights = jnp.where(row == 0, first, jnp.where(row == 1, second, jnp.where(row == 2, third, 0.0)))
    numbers = jnp.concatenate([high, low], axis=0).astype(F32)
    gap = jnp.zeros((16, 16), F32)
    return jnp.concatenate([numbers, gap, weights, gap], axis=1).astype(BF16)


def unpack_rows(packed):
    tiles = [packed[n].astype(F32) for n in range(32)]
    numbers = jnp.concatenate([t[:, :ROWS] for t in tiles], axis=1)
    weights = jnp.concatenate([t[:, 64 : 64 + ROWS] for t in tiles], axis=1)
    ids = (numbers[:POS] * 256.0 + numbers[POS:]).astype(jnp.int32)
    return ids, 0.5 * (weights[0:1] + weights[1:2] + weights[2:3])


def kernel(
    queries,
    positives,
    weight,
    labels,
    query_grad,
    weight_grad,
    q,
    far_q,
    packed,
    far_packed,
    w,
    qg,
    wg,
    g,
    far_g,
    bits,
    half_weight,
    far_bits,
    far_weight,
    my_positives,
    my_weight,
    zs,
    zr,
    sib_s,
    sib_r,
    one_s,
    one_r,
    two_s,
    two_r,
    load_sem,
    send_sem,
    recv_sem,
):
    l, d = lax.axis_index("label"), lax.axis_index("dp")
    x, y, z, c = l % 4, (l // 4) * 2 + (d // 2) % 2, d // 4, d % 2
    yc = d % 4
    a, b = jnp.where(c == 0, x, y), jnp.where(c == 0, y, x)

    def device(x, y, z, c):
        return ((y // 2) * 4 + x, z * 4 + (y % 2) * 2 + c)

    def in_plane(a, b):
        return device(jnp.where(c == 0, a, b), jnp.where(c == 0, b, a), z, c)

    def turn(v, k):
        return (v + k + 4) % 4

    def plane_at(away):
        return (z + jnp.where(c == 0, away + 8, 8 - away)) % 8

    to_a = [in_plane(turn(a, k), b) for k in RING[:3]]
    to_b = [in_plane(a, turn(b, k)) for k in RING[:3]]
    to_z = [device(x, y, plane_at(k), c) for k in (1, -1)]
    opposite = device(x, y, plane_at(4), c)
    sibling = device(x, y, z, 1 - c)

    barrier = pltpu.get_barrier_semaphore()
    for partner in (*to_a, *to_b, *to_z, opposite, sibling):
        pl.semaphore_signal(barrier, inc=1, device_id=partner, device_id_type=MESH)

    def tile(r, h, i):
        return (r * 2 + h) * 4 + i

    def place(r, h, i, count=1):
        return pl.ds(tile(r, h, i) * ROWS, count * ROWS)

    own, own_tile = place(HOME, 0, HOME), tile(HOME, 0, HOME)
    loads = [
        pltpu.make_async_copy(queries, q.at[own], load_sem.at[0]),
        pltpu.make_async_copy(positives, my_positives, load_sem.at[1]),
        pltpu.make_async_copy(weight, my_weight, load_sem.at[2]),
    ]
    for j, away in enumerate(AWAY):
        start = pl.multiple_of((plane_at(away) * 4 + yc) * LAB, LAB)
        loads.append(
            pltpu.make_async_copy(
                labels.at[pl.ds(start, LAB)], w.at[pl.ds(j * LAB, LAB)], load_sem.at[3 + j]
            )
        )
    for load in loads:
        load.start()
    for load in loads[:3]:
        load.wait()
    packed[own_tile] = pack_rows(my_positives[...], my_weight[...])
    pl.semaphore_wait(barrier, 10)

    copies = []

    def prepare(src, dst, to):
        i = len(copies)
        copy = pltpu.make_async_remote_copy(
            src_ref=src,
            dst_ref=dst,
            send_sem=send_sem.at[i],
            recv_sem=recv_sem.at[i],
            device_id=to,
            device_id_type=MESH,
        )
        copies.append(copy)
        return copy

    def send(src, dst, to):
        copy = prepare(src, dst, to)
        copy.start()
        return copy

    def start(group):
        for copy in group:
            copy.start()

    def arrive(group):
        for copy in group:
            copy.wait_recv()

    class Gather:
        def __init__(self, q, packed):
            def rows(src, dst, to):
                return prepare(q.at[place(*src)], q.at[place(*dst)], to)

            def tiles(src, dst, count, to):
                return prepare(
                    packed.at[pl.ds(tile(*src), count)], packed.at[pl.ds(tile(*dst), count)], to
                )

            here = (HOME, 0, HOME)
            self.own_a = [rows(here, (HOME, 0, BACK[r]), to_a[r]) for r in range(3)]
            self.own_tiles = [tiles(here, (HOME, 0, BACK[r]), 1, to_a[r]) for r in range(3)]
            self.to_b = [
                [rows((HOME, 0, i), (BACK[r], 0, i), to_b[r]) for i in range(4)] for r in range(3)
            ]
            self.b_tiles = [tiles((HOME, 0, 0), (BACK[r], 0, 0), 4, to_b[r]) for r in range(3)]
            self.across = [
                [rows((r, 0, i), (r, 1, i), sibling) for i in range(4)] for r in range(4)
            ]
            self.all_tiles = [tiles((r, 0, 0), (r, 1, 0), 4, sibling) for r in range(4)]

        def first(self):
            start(self.own_tiles)
            start(self.own_a)
            for r in (1, 2, 0):
                self.to_b[r][HOME].start()
            self.across[HOME][HOME].start()

        def second(self):
            arrive(self.own_tiles)
            start(self.b_tiles)
            for i in (1, 2, 0):
                self.own_a[BACK[i]].wait_recv()
                self.to_b[1][i].start()
                self.to_b[2][i].start()
                self.across[HOME][i].start()
            for i in (1, 2, 0):
                self.to_b[0][i].start()

        def share_tiles(self):
            arrive(self.b_tiles)
            start(self.all_tiles)

        def share(self, r):
            for i in (3, 1, 2, 0):
                self.to_b[BACK[r]][i].wait_recv()
                self.across[r][i].start()

    near, far = Gather(q, packed), Gather(far_q, far_packed)
    near.first()
    exchange = [
        send(q.at[own], far_q.at[own], opposite),
        send(packed.at[own_tile], far_packed.at[own_tile], opposite),
    ]

    sub = lax.broadcasted_iota(jnp.int32, (8, PLANE), 0)

    def unpack(packed, weights, held, blocks):
        ids, halves = unpack_rows(packed)
        weights[...] = jnp.broadcast_to(halves, (8, PLANE))
        label = ids - l * (4 * NZ * LAB)
        mine = (label >= 0) & (label < 4 * NZ * LAB) & (((label >> 8) & 3) == yc)
        word = jnp.where(mine, (label >> 10) * 8 + (label & 7), -1)
        bit = lax.shift_left(jnp.int32(1), (label >> 3) & 31)
        for n, j in enumerate(blocks):
            words = jnp.zeros((8, PLANE), jnp.int32)
            for s in range(POS):
                hit = word[s : s + 1] == plane_at(AWAY[j]) * 8 + sub
                words = words | jnp.where(hit, bit[s : s + 1], 0)
            held[n] = words

    def block(j, count):
        return pl.ds(j * LAB, count * LAB)

    def gradient(j, count, rows, held, scale):
        logits = lax.dot_general(
            w[block(j, count), :], rows, (((1,), (1,)), ((), ())), preferred_element_type=F32
        )
        parts = []
        for n in range(count):
            for k in range(LAB // 8):
                mask = jnp.int32(1 << k if k < 31 else -(1 << 31))
                target = jnp.where((held[n] & mask) != 0, -1.0, 1.0)
                at = n * LAB + 8 * k
                parts.append(scale * (jnp.tanh(0.5 * logits[at : at + 8]) + target))
        return jnp.concatenate(parts, axis=0).astype(BF16)

    def forward(j, count, rows, first=False):
        held = [bits[j + n, :, rows] for n in range(count)]
        out = g.at[pl.ds(0, count * LAB), rows]
        out[...] = gradient(j, count, q[rows, :], held, half_weight[:, rows])
        part = lax.dot_general(
            out[...], w[block(j, count), :], (((0,), (0,)), ((), ())), preferred_element_type=F32
        )
        if first:
            qg[rows, :] = part
        else:
            qg[rows, :] += part

    def backward(j, count, rows, first):
        part = jnp.dot(g[pl.ds(0, count * LAB), rows], q[rows, :], preferred_element_type=F32)
        if first:
            wg[block(j, count), :] = part
        else:
            wg[block(j, count), :] += part

    def far_backward(j, count):
        out = far_g.at[pl.ds(0, count * LAB)]
        held = [far_bits[j - 2 + n] for n in range(count)]
        out[...] = gradient(j, count, far_q[...], held, far_weight[...])
        wg[block(j, count), :] += jnp.dot(out[...], far_q[...], preferred_element_type=F32)

    everyone = pl.ds(0, PLANE)

    def chunk(r):
        return pl.ds(r * CHUNK, CHUNK)

    near.second()
    arrive(exchange)
    far.first()
    near.share_tiles()
    arrive(near.all_tiles)
    unpack(packed, half_weight, bits, range(8))
    for load in loads[3:]:
        load.wait()
    for n, r in enumerate((HOME, 1, 2, 0)):
        arrive(near.across[r])
        forward(0, 2, chunk(r), first=True)
        backward(0, 2, chunk(r), first=n == 0)
        if n == 0:
            for k in (1, 2, 0):
                near.share(k)
        if n == 2:
            far.second()

    passes = [[prepare(zs.at[t, m], zr.at[t, m], to_z[t]) for m in range(4)] for t in range(2)]

    def pass_on(m, way):
        total = wg[pl.ds((2 * (m // 2) + way) * LAB + m % 2 * HALF, HALF), :]
        if m >= 2:
            passes[way][m - 2].wait_recv()
            total = total + zr[way, m - 2].astype(F32)
        zs[way, m] = total.astype(BF16)
        passes[way][m].start()

    for m in range(2):
        pass_on(m, 0)
        pass_on(m, 1)

    forward(2, 1, everyone)
    backward(2, 1, everyone, first=True)
    forward(3, 1, everyone)
    backward(3, 1, everyone, first=True)

    crossed, along_b, along_a = [], [], []

    def cross(r):
        sib_s[r] = qg[place(r, 1, 0, 4), :].astype(BF16)
        crossed.append(send(sib_s.at[r], sib_r.at[r], sibling))

    def go_b(r):
        crossed[r].wait_recv()
        rows = place(r, 0, 0, 4)
        total = qg[rows, :] + sib_r[r].astype(F32)
        if r == HOME:
            qg[rows, :] = total
        else:
            one_s[r] = total.astype(BF16)
            along_b.append(send(one_s.at[r], one_r.at[r], to_b[r]))

    for r in range(3):
        forward(4, 4, chunk(r))
        cross(r)
        if r > 0:
            go_b(r - 1)
        if r == 0:
            far.share_tiles()
        if r == 1:
            for k in (1, 2, 0):
                far.share(k)
    arrive(far.all_tiles)
    unpack(far_packed, far_weight, far_bits, (2, 3, 4))
    for r in range(4):
        arrive(far.across[r])
    for way in range(2):
        far_backward(2 + way, 1)
        pass_on(2, way)
        pass_on(3, way)
        if way == 0:
            go_b(2)
    forward(4, 4, chunk(HOME))
    cross(HOME)
    backward(4, 1, everyone, first=True)
    far_backward(4, 1)
    go_b(HOME)

    arrive(along_b)
    for i in range(4):
        part = pl.ds(i * ROWS, ROWS)
        total = qg[place(HOME, 0, i), :]
        for r in range(3):
            total = total + one_r[r, part, :].astype(F32)
        if i == HOME:
            query_grad[...] = total
        else:
            two_s[i] = total.astype(BF16)
            along_a.append(send(two_s.at[i], two_r.at[i], to_a[i]))
    for m in (2, 3):
        half = pl.ds((m - 2) * HALF, HALF)
        total = wg[pl.ds(4 * LAB + (m - 2) * HALF, HALF), :]
        for way in range(2):
            passes[way][m].wait_recv()
            total = total + zr[way, m].astype(F32)
        weight_grad[half, :] = total
    for i in range(3):
        along_a[i].wait_recv()
        query_grad[...] += two_r[i].astype(F32)

    for copy in copies:
        copy.wait_send()


COPIES = 2 * 41 + 2 * 3 + 2 + 8 + 4 + 3 + 3


def hand_over(query_in, weight_in, query_out, weight_out):
    query_out[...] = query_in[...]
    weight_out[...] = weight_in[...]


def on_device(queries, positives, row_weight, label_weight):
    vmem = pl.BlockSpec(memory_space=pltpu.VMEM)
    hbm = pl.BlockSpec(memory_space=pl.ANY)
    outs = (jax.ShapeDtypeStruct((ROWS, D), F32), jax.ShapeDtypeStruct((LAB, D), F32))
    grads = pl.pallas_call(
        kernel,
        out_shape=outs,
        in_specs=[hbm, hbm, hbm, hbm],
        out_specs=(vmem, vmem),
        scratch_shapes=[
            pltpu.VMEM((PLANE, D), BF16),
            pltpu.VMEM((PLANE, D), BF16),
            pltpu.VMEM((32, 16, 128), BF16),
            pltpu.VMEM((32, 16, 128), BF16),
            pltpu.VMEM((NZ * LAB, D), BF16),
            pltpu.VMEM((PLANE, D), F32),
            pltpu.VMEM((5 * LAB, D), F32),
            pltpu.VMEM((4 * LAB, PLANE), BF16),
            pltpu.VMEM((2 * LAB, PLANE), BF16),
            pltpu.VMEM((NZ, 8, PLANE), jnp.int32),
            pltpu.VMEM((8, PLANE), F32),
            pltpu.VMEM((3, 8, PLANE), jnp.int32),
            pltpu.VMEM((8, PLANE), F32),
            pltpu.VMEM((POS, ROWS), jnp.int32),
            pltpu.VMEM((1, ROWS), F32),
            pltpu.VMEM((2, 4, HALF, D), BF16),
            pltpu.VMEM((2, 4, HALF, D), BF16),
            pltpu.VMEM((4, 4 * ROWS, D), BF16),
            pltpu.VMEM((4, 4 * ROWS, D), BF16),
            pltpu.VMEM((3, 4 * ROWS, D), BF16),
            pltpu.VMEM((3, 4 * ROWS, D), BF16),
            pltpu.VMEM((3, ROWS, D), BF16),
            pltpu.VMEM((3, ROWS, D), BF16),
            pltpu.SemaphoreType.DMA((NZ + 3,)),
            pltpu.SemaphoreType.DMA((COPIES,)),
            pltpu.SemaphoreType.DMA((COPIES,)),
        ],
        compiler_params=pltpu.CompilerParams(
            collective_id=0, has_side_effects=True, vmem_limit_bytes=56 * 2**20
        ),
        cost_estimate=pl.CostEstimate(
            flops=6 * PLANE * NZ * LAB * D, bytes_accessed=NZ * LAB * D * 2, transcendentals=0
        ),
    )(queries, positives.T, row_weight[None, :], label_weight)
    return pl.pallas_call(
        hand_over,
        out_shape=outs,
        in_specs=[vmem, vmem],
        out_specs=(vmem, vmem),
        compiler_params=pltpu.CompilerParams(vmem_limit_bytes=56 * 2**20),
    )(*grads)


def solution(mesh):
    placed = (
        P(("label", "dp"), None),
        P(("label", "dp"), None),
        P(("label", "dp")),
        P("label", None),
    )
    return jax.shard_map(
        on_device,
        mesh=mesh,
        in_specs=placed,
        out_specs=(P(("label", "dp"), None), P(("label", "dp"), None)),
        check_vma=False,
    )
```

```python
import functools

import jax
import jax.numpy as jnp
from jax import lax
from jax.experimental import pallas as pl
from jax.experimental.pallas import tpu as pltpu
from jax.sharding import PartitionSpec as P

MESH = pl.DeviceIdType.MESH
BF16, F32 = jnp.bfloat16, jnp.float32

ROWS, D, POS = 48, 768, 8
PLANE = 32 * ROWS
LAB, NZ = 256, 8
HALF = LAB // 2
CHUNK = 8 * ROWS
RING = (2, 1, -1, 0)
BACK = (0, 2, 1, 3)
HOME = 3
AWAY = (2, -2, 1, -1, 0, 3, -3, 4)


def pack_rows(positives, weight):
    high, low = positives >> 8, positives & 255
    first = weight.astype(BF16).astype(F32)
    rest = weight - first
    second = rest.astype(BF16).astype(F32)
    third = rest - second
    row = lax.broadcasted_iota(jnp.int32, (16, ROWS), 0)
    weights = jnp.where(row == 0, first, jnp.where(row == 1, second, jnp.where(row == 2, third, 0.0)))
    numbers = jnp.concatenate([high, low], axis=0).astype(F32)
    gap = jnp.zeros((16, 16), F32)
    return jnp.concatenate([numbers, gap, weights, gap], axis=1).astype(BF16)


def unpack_rows(packed, lo, hi):
    tiles = [packed[n].astype(F32) for n in range(lo, hi)]
    numbers = jnp.concatenate([t[:, :ROWS] for t in tiles], axis=1)
    weights = jnp.concatenate([t[:, 64 : 64 + ROWS] for t in tiles], axis=1)
    ids = (numbers[:POS] * 256.0 + numbers[POS:]).astype(jnp.int32)
    return ids, 0.5 * (weights[0:1] + weights[1:2] + weights[2:3])


def kernel(
    queries,
    positives,
    weight,
    labels,
    query_grad,
    weight_grad,
    q,
    far_q,
    packed,
    far_packed,
    w,
    qg,
    wg,
    g,
    far_g,
    bits,
    half_weight,
    far_bits,
    far_weight,
    my_positives,
    my_weight,
    zs,
    zr,
    sib_s,
    sib_r,
    one_s,
    one_r,
    two_s,
    two_r,
    load_sem,
    send_sem,
    recv_sem,
):
    l, d = lax.axis_index("label"), lax.axis_index("dp")
    x, y, z, c = l % 4, (l // 4) * 2 + (d // 2) % 2, d // 4, d % 2
    yc = d % 4
    a, b = jnp.where(c == 0, x, y), jnp.where(c == 0, y, x)

    def device(x, y, z, c):
        return ((y // 2) * 4 + x, z * 4 + (y % 2) * 2 + c)

    def in_plane(a, b):
        return device(jnp.where(c == 0, a, b), jnp.where(c == 0, b, a), z, c)

    def turn(v, k):
        return (v + k + 4) % 4

    def plane_at(away):
        return (z + jnp.where(c == 0, away + 8, 8 - away)) % 8

    to_a = [in_plane(turn(a, k), b) for k in RING[:3]]
    to_b = [in_plane(a, turn(b, k)) for k in RING[:3]]
    to_z = [device(x, y, plane_at(k), c) for k in (1, -1)]
    opposite = device(x, y, plane_at(4), c)
    sibling = device(x, y, z, 1 - c)

    barrier = pltpu.get_barrier_semaphore()
    for partner in (*to_a, *to_b, *to_z, opposite, sibling):
        pl.semaphore_signal(barrier, inc=1, device_id=partner, device_id_type=MESH)

    def tile(r, h, i):
        return (r * 2 + h) * 4 + i

    def place(r, h, i, count=1):
        return pl.ds(tile(r, h, i) * ROWS, count * ROWS)

    own, own_tile = place(HOME, 0, HOME), tile(HOME, 0, HOME)
    loads = [
        pltpu.make_async_copy(queries, q.at[own], load_sem.at[0]),
        pltpu.make_async_copy(positives, my_positives, load_sem.at[1]),
        pltpu.make_async_copy(weight, my_weight, load_sem.at[2]),
    ]
    for j, away in enumerate(AWAY):
        start = pl.multiple_of((plane_at(away) * 4 + yc) * LAB, LAB)
        loads.append(
            pltpu.make_async_copy(
                labels.at[pl.ds(start, LAB)], w.at[pl.ds(j * LAB, LAB)], load_sem.at[3 + j]
            )
        )
    for load in loads:
        load.start()
    for load in loads[:3]:
        load.wait()
    packed[own_tile] = pack_rows(my_positives[...], my_weight[...])
    pl.semaphore_wait(barrier, 10)

    copies = []

    def prepare(src, dst, to):
        i = len(copies)
        copy = pltpu.make_async_remote_copy(
            src_ref=src,
            dst_ref=dst,
            send_sem=send_sem.at[i],
            recv_sem=recv_sem.at[i],
            device_id=to,
            device_id_type=MESH,
        )
        copies.append(copy)
        return copy

    def send(src, dst, to):
        copy = prepare(src, dst, to)
        copy.start()
        return copy

    def start(group):
        for copy in group:
            copy.start()

    def arrive(group):
        for copy in group:
            copy.wait_recv()

    class Gather:
        def __init__(self, q, packed):
            def rows(src, dst, count, to):
                return prepare(q.at[place(*src, count)], q.at[place(*dst, count)], to)

            def tiles(src, dst, count, to):
                return prepare(
                    packed.at[pl.ds(tile(*src), count)], packed.at[pl.ds(tile(*dst), count)], to
                )

            here = (HOME, 0, HOME)
            self.own_a = [rows(here, (HOME, 0, BACK[r]), 1, to_a[r]) for r in range(3)]
            self.own_tiles = [tiles(here, (HOME, 0, BACK[r]), 1, to_a[r]) for r in range(3)]
            self.to_b = [
                [rows((HOME, 0, i), (BACK[r], 0, i), n, to_b[r]) for i, n in ((3, 1), (1, 2), (0, 1))]
                for r in range(3)
            ]
            self.b_tiles = [tiles((HOME, 0, 0), (BACK[r], 0, 0), 4, to_b[r]) for r in range(3)]
            self.across = [[rows((r, 0, 0), (r, 1, 0), 4, sibling)] for r in range(3)]
            self.across.append(
                [rows(here, (HOME, 1, HOME), 1, sibling), rows((HOME, 0, 0), (HOME, 1, 0), 3, sibling)]
            )
            self.all_tiles = [tiles((r, 0, 0), (r, 1, 0), 4, sibling) for r in range(4)]

        def first(self):
            start(self.own_tiles)
            start(self.own_a)
            for r in (1, 2, 0):
                self.to_b[r][0].start()
            self.across[HOME][0].start()

        def second(self):
            arrive(self.own_tiles)
            self.all_tiles[HOME].start()
            start(self.b_tiles)
            self.own_a[1].wait_recv()
            self.own_a[2].wait_recv()
            for r in (1, 2, 0):
                self.to_b[r][1].start()
            self.own_a[0].wait_recv()
            for r in (1, 2, 0):
                self.to_b[r][2].start()
            self.across[HOME][1].start()

        def share_tiles(self):
            arrive(self.b_tiles)
            start(self.all_tiles[:HOME])

        def share(self, r):
            arrive(self.to_b[BACK[r]])
            start(self.across[r])

    near, far = Gather(q, packed), Gather(far_q, far_packed)
    near.first()
    exchange = [
        send(q.at[own], far_q.at[own], opposite),
        send(packed.at[own_tile], far_packed.at[own_tile], opposite),
    ]

    def unpack(packed, weights, held, blocks, lo, hi):
        ids, halves = unpack_rows(packed, lo, hi)
        rows, count = pl.ds(lo * ROWS, (hi - lo) * ROWS), (hi - lo) * ROWS
        sub = lax.broadcasted_iota(jnp.int32, (8, count), 0)
        weights[:, rows] = jnp.broadcast_to(halves, (8, count))
        label = ids - l * (4 * NZ * LAB)
        mine = (label >= 0) & (label < 4 * NZ * LAB) & (((label >> 8) & 3) == yc)
        word = jnp.where(mine, (label >> 10) * 8 + (label & 7), -1)
        bit = lax.shift_left(jnp.int32(1), (label >> 3) & 31)
        for n, j in enumerate(blocks):
            words = jnp.zeros((8, count), jnp.int32)
            for s in range(POS):
                hit = word[s : s + 1] == plane_at(AWAY[j]) * 8 + sub
                words = words | jnp.where(hit, bit[s : s + 1], 0)
            held[n, :, rows] = words

    def block(j, count):
        return pl.ds(j * LAB, count * LAB)

    def gradient(j, count, rows, held, scale):
        logits = lax.dot_general(
            w[block(j, count), :], rows, (((1,), (1,)), ((), ())), preferred_element_type=F32
        )
        parts = []
        for n in range(count):
            for k in range(LAB // 8):
                mask = jnp.int32(1 << k if k < 31 else -(1 << 31))
                target = jnp.where((held[n] & mask) != 0, -1.0, 1.0)
                at = n * LAB + 8 * k
                parts.append(scale * (jnp.tanh(0.5 * logits[at : at + 8]) + target))
        return jnp.concatenate(parts, axis=0).astype(BF16)

    def forward(j, count, rows, out, first=False):
        held = [bits[j + n, :, rows] for n in range(count)]
        out[...] = gradient(j, count, q[rows, :], held, half_weight[:, rows])
        part = lax.dot_general(
            out[...], w[block(j, count), :], (((0,), (0,)), ((), ())), preferred_element_type=F32
        )
        if first:
            qg[rows, :] = part
        else:
            qg[rows, :] += part

    def backward(j, count, rows, grads, first=False):
        part = jnp.dot(grads[...], q[rows, :], preferred_element_type=F32)
        if first:
            wg[block(j, count), :] = part
        else:
            wg[block(j, count), :] += part

    def far_backward(j, count):
        out = far_g.at[pl.ds(0, count * LAB)]
        held = [far_bits[j - 2 + n] for n in range(count)]
        out[...] = gradient(j, count, far_q[...], held, far_weight[...])
        wg[block(j, count), :] += jnp.dot(out[...], far_q[...], preferred_element_type=F32)

    def chunk(r):
        return pl.ds(r * CHUNK, CHUNK)

    def grads_of(count, rows):
        return g.at[pl.ds(0, count * LAB), rows]

    others, everyone = pl.ds(0, HOME * CHUNK), pl.ds(0, PLANE)
    crossed, along_b, along_a = [None] * 4, [], []

    def cross(r):
        sib_s[r] = qg[place(r, 1, 0, 4), :].astype(BF16)
        crossed[r] = send(sib_s.at[r], sib_r.at[r], sibling)

    def go_b(r):
        crossed[r].wait_recv()
        rows = place(r, 0, 0, 4)
        total = qg[rows, :] + sib_r[r].astype(F32)
        if r == HOME:
            qg[rows, :] = total
        else:
            one_s[r] = total.astype(BF16)
            along_b.append(send(one_s.at[r], one_r.at[r], to_b[r]))

    near.second()
    arrive(exchange)
    far.first()
    near.all_tiles[HOME].wait_recv()
    unpack(packed, half_weight, bits, range(8), 24, 32)
    for load in loads[3:]:
        load.wait()
    arrive(near.across[HOME])
    forward(0, 4, chunk(HOME), grads_of(4, chunk(HOME)), first=True)
    backward(0, 4, chunk(HOME), grads_of(4, chunk(HOME)), first=True)
    near.share_tiles()
    near.share(1)
    near.share(2)
    arrive(near.all_tiles[:HOME])
    unpack(packed, half_weight, bits, range(8), 0, 24)
    for r in (1, 2, 0):
        if r == 2:
            near.share(0)
            far.second()
        arrive(near.across[r])
        grads = grads_of(2, chunk(r))
        forward(0, 2, chunk(r), grads, first=True)
        backward(0, 2, chunk(r), grads)

    passes = [[prepare(zs.at[t, m], zr.at[t, m], to_z[t]) for m in range(4)] for t in range(2)]

    def pass_on(m, way):
        total = wg[pl.ds((2 * (m // 2) + way) * LAB + m % 2 * HALF, HALF), :]
        if m >= 2:
            passes[way][m - 2].wait_recv()
            total = total + zr[way, m - 2].astype(F32)
        zs[way, m] = total.astype(BF16)
        passes[way][m].start()

    for m in range(2):
        pass_on(m, 0)
        pass_on(m, 1)

    for j in (2, 3):
        forward(j, 1, others, grads_of(1, others))
        backward(j, 1, others, grads_of(1, others))

    for r in range(3):
        forward(4, 4, chunk(r), grads_of(4, chunk(r)))
        cross(r)
        if r > 0:
            go_b(r - 1)
        if r == 0:
            far.share_tiles()
        if r == 1:
            for k in (1, 2, 0):
                far.share(k)
    arrive(far.all_tiles)
    unpack(far_packed, far_weight, far_bits, (2, 3, 4), 0, 32)
    for r in range(4):
        arrive(far.across[r])
    for way in range(2):
        far_backward(2 + way, 1)
        pass_on(2, way)
        pass_on(3, way)
        if way == 0:
            go_b(2)
    forward(4, 4, chunk(HOME), grads_of(4, chunk(HOME)))
    cross(HOME)
    backward(4, 1, everyone, grads_of(1, everyone), first=True)
    go_b(HOME)

    for copy in copies[:GATHERED]:
        copy.wait_send()
    arrive(along_b)
    for i in range(4):
        part = pl.ds(i * ROWS, ROWS)
        total = qg[place(HOME, 0, i), :]
        for r in range(3):
            total = total + one_r[r, part, :].astype(F32)
        if i == HOME:
            query_grad[...] = total
        else:
            two_s[i] = total.astype(BF16)
            along_a.append(send(two_s.at[i], two_r.at[i], to_a[i]))
    far_backward(4, 1)
    for m in (2, 3):
        half = pl.ds((m - 2) * HALF, HALF)
        total = wg[pl.ds(4 * LAB + (m - 2) * HALF, HALF), :]
        for way in range(2):
            passes[way][m].wait_recv()
            total = total + zr[way, m].astype(F32)
        weight_grad[half, :] = total
    for i in range(3):
        along_a[i].wait_recv()
        query_grad[...] += two_r[i].astype(F32)

    for copy in copies[GATHERED:]:
        copy.wait_send()


GATHERED = 2 * 27 + 2
COPIES = GATHERED + 8 + 4 + 3 + 3


def hand_over(query_in, weight_in, query_out, weight_out):
    query_out[...] = query_in[...]
    weight_out[...] = weight_in[...]


def on_device(queries, positives, row_weight, label_weight):
    vmem = pl.BlockSpec(memory_space=pltpu.VMEM)
    hbm = pl.BlockSpec(memory_space=pl.ANY)
    outs = (jax.ShapeDtypeStruct((ROWS, D), F32), jax.ShapeDtypeStruct((LAB, D), F32))
    grads = pl.pallas_call(
        kernel,
        out_shape=outs,
        in_specs=[hbm, hbm, hbm, hbm],
        out_specs=(vmem, vmem),
        scratch_shapes=[
            pltpu.VMEM((PLANE, D), BF16),
            pltpu.VMEM((PLANE, D), BF16),
            pltpu.VMEM((32, 16, 128), BF16),
            pltpu.VMEM((32, 16, 128), BF16),
            pltpu.VMEM((NZ * LAB, D), BF16),
            pltpu.VMEM((PLANE, D), F32),
            pltpu.VMEM((5 * LAB, D), F32),
            pltpu.VMEM((4 * LAB, PLANE), BF16),
            pltpu.VMEM((LAB, PLANE), BF16),
            pltpu.VMEM((NZ, 8, PLANE), jnp.int32),
            pltpu.VMEM((8, PLANE), F32),
            pltpu.VMEM((3, 8, PLANE), jnp.int32),
            pltpu.VMEM((8, PLANE), F32),
            pltpu.VMEM((POS, ROWS), jnp.int32),
            pltpu.VMEM((1, ROWS), F32),
            pltpu.VMEM((2, 4, HALF, D), BF16),
            pltpu.VMEM((2, 4, HALF, D), BF16),
            pltpu.VMEM((4, 4 * ROWS, D), BF16),
            pltpu.VMEM((4, 4 * ROWS, D), BF16),
            pltpu.VMEM((3, 4 * ROWS, D), BF16),
            pltpu.VMEM((3, 4 * ROWS, D), BF16),
            pltpu.VMEM((3, ROWS, D), BF16),
            pltpu.VMEM((3, ROWS, D), BF16),
            pltpu.SemaphoreType.DMA((NZ + 3,)),
            pltpu.SemaphoreType.DMA((COPIES,)),
            pltpu.SemaphoreType.DMA((COPIES,)),
        ],
        compiler_params=pltpu.CompilerParams(
            collective_id=0, has_side_effects=True, vmem_limit_bytes=56 * 2**20
        ),
        cost_estimate=pl.CostEstimate(
            flops=6 * PLANE * NZ * LAB * D, bytes_accessed=NZ * LAB * D * 2, transcendentals=0
        ),
    )(queries, positives.T, row_weight[None, :], label_weight)
    return pl.pallas_call(
        hand_over,
        out_shape=outs,
        in_specs=[vmem, vmem],
        out_specs=(vmem, vmem),
        compiler_params=pltpu.CompilerParams(vmem_limit_bytes=56 * 2**20),
    )(*grads)


def solution(mesh):
    placed = (
        P(("label", "dp"), None),
        P(("label", "dp"), None),
        P(("label", "dp")),
        P("label", None),
    )
    return jax.shard_map(
        on_device,
        mesh=mesh,
        in_specs=placed,
        out_specs=(P(("label", "dp"), None), P(("label", "dp"), None)),
        check_vma=False,
    )
```

```python
import functools

import jax
import jax.numpy as jnp
from jax import lax
from jax.experimental import pallas as pl
from jax.experimental.pallas import tpu as pltpu
from jax.sharding import PartitionSpec as P

MESH = pl.DeviceIdType.MESH
BF16, F32 = jnp.bfloat16, jnp.float32

ROWS, D, POS = 48, 768, 8
PLANE = 32 * ROWS
LAB, NZ = 256, 8
HALF = LAB // 2
CHUNK = 8 * ROWS
RING = (2, 1, -1, 0)
BACK = (0, 2, 1, 3)
HOME = 3
AWAY = (2, -2, 1, -1, 0, 3, -3, 4)


def pack_rows(positives, weight):
    high, low = positives >> 8, positives & 255
    first = weight.astype(BF16).astype(F32)
    rest = weight - first
    second = rest.astype(BF16).astype(F32)
    third = rest - second
    row = lax.broadcasted_iota(jnp.int32, (16, ROWS), 0)
    weights = jnp.where(row == 0, first, jnp.where(row == 1, second, jnp.where(row == 2, third, 0.0)))
    numbers = jnp.concatenate([high, low], axis=0).astype(F32)
    gap = jnp.zeros((16, 16), F32)
    return jnp.concatenate([numbers, gap, weights, gap], axis=1).astype(BF16)


def unpack_rows(packed, lo, hi):
    tiles = [packed[n].astype(F32) for n in range(lo, hi)]
    numbers = jnp.concatenate([t[:, :ROWS] for t in tiles], axis=1)
    weights = jnp.concatenate([t[:, 64 : 64 + ROWS] for t in tiles], axis=1)
    ids = (numbers[:POS] * 256.0 + numbers[POS:]).astype(jnp.int32)
    return ids, 0.5 * (weights[0:1] + weights[1:2] + weights[2:3])


def kernel(
    queries,
    positives,
    weight,
    labels,
    query_out,
    weight_out,
    query_grad,
    weight_grad,
    out_sem,
    q,
    far_q,
    packed,
    far_packed,
    w,
    qg,
    wg,
    g,
    far_g,
    bits,
    half_weight,
    far_bits,
    far_weight,
    my_positives,
    my_weight,
    zs,
    zr,
    sib_s,
    sib_r,
    one_s,
    one_r,
    two_s,
    two_r,
    load_sem,
    send_sem,
    recv_sem,
):
    l, d = lax.axis_index("label"), lax.axis_index("dp")
    x, y, z, c = l % 4, (l // 4) * 2 + (d // 2) % 2, d // 4, d % 2
    yc = d % 4
    a, b = jnp.where(c == 0, x, y), jnp.where(c == 0, y, x)

    def device(x, y, z, c):
        return ((y // 2) * 4 + x, z * 4 + (y % 2) * 2 + c)

    def in_plane(a, b):
        return device(jnp.where(c == 0, a, b), jnp.where(c == 0, b, a), z, c)

    def turn(v, k):
        return (v + k + 4) % 4

    def plane_at(away):
        return (z + jnp.where(c == 0, away + 8, 8 - away)) % 8

    to_a = [in_plane(turn(a, k), b) for k in RING[:3]]
    to_b = [in_plane(a, turn(b, k)) for k in RING[:3]]
    to_z = [device(x, y, plane_at(k), c) for k in (1, -1)]
    opposite = device(x, y, plane_at(4), c)
    sibling = device(x, y, z, 1 - c)

    barrier = pltpu.get_barrier_semaphore()
    for partner in (*to_a, *to_b, *to_z, opposite, sibling):
        pl.semaphore_signal(barrier, inc=1, device_id=partner, device_id_type=MESH)

    def tile(r, h, i):
        return (r * 2 + h) * 4 + i

    def place(r, h, i, count=1):
        return pl.ds(tile(r, h, i) * ROWS, count * ROWS)

    own, own_tile = place(HOME, 0, HOME), tile(HOME, 0, HOME)
    loads = [
        pltpu.make_async_copy(queries, q.at[own], load_sem.at[0]),
        pltpu.make_async_copy(positives, my_positives, load_sem.at[1]),
        pltpu.make_async_copy(weight, my_weight, load_sem.at[2]),
    ]
    for j, away in enumerate(AWAY):
        start = pl.multiple_of((plane_at(away) * 4 + yc) * LAB, LAB)
        loads.append(
            pltpu.make_async_copy(
                labels.at[pl.ds(start, LAB)], w.at[pl.ds(j * LAB, LAB)], load_sem.at[3 + j]
            )
        )
    for load in loads:
        load.start()
    for load in loads[:3]:
        load.wait()
    packed[own_tile] = pack_rows(my_positives[...], my_weight[...])
    pl.semaphore_wait(barrier, 10)

    copies = []

    def prepare(src, dst, to):
        i = len(copies)
        copy = pltpu.make_async_remote_copy(
            src_ref=src,
            dst_ref=dst,
            send_sem=send_sem.at[i],
            recv_sem=recv_sem.at[i],
            device_id=to,
            device_id_type=MESH,
        )
        copies.append(copy)
        return copy

    def send(src, dst, to):
        copy = prepare(src, dst, to)
        copy.start()
        return copy

    def start(group):
        for copy in group:
            copy.start()

    def arrive(group):
        for copy in group:
            copy.wait_recv()

    class Gather:
        def __init__(self, q, packed):
            def rows(src, dst, count, to):
                return prepare(q.at[place(*src, count)], q.at[place(*dst, count)], to)

            def tiles(src, dst, count, to):
                return prepare(
                    packed.at[pl.ds(tile(*src), count)], packed.at[pl.ds(tile(*dst), count)], to
                )

            here = (HOME, 0, HOME)
            self.own_a = [rows(here, (HOME, 0, BACK[r]), 1, to_a[r]) for r in range(3)]
            self.own_tiles = [tiles(here, (HOME, 0, BACK[r]), 1, to_a[r]) for r in range(3)]
            self.to_b = [
                [rows((HOME, 0, i), (BACK[r], 0, i), n, to_b[r]) for i, n in ((3, 1), (1, 2), (0, 1))]
                for r in range(3)
            ]
            self.b_tiles = [tiles((HOME, 0, 0), (BACK[r], 0, 0), 4, to_b[r]) for r in range(3)]
            self.across = [[rows((r, 0, 0), (r, 1, 0), 4, sibling)] for r in range(3)]
            self.across.append(
                [rows(here, (HOME, 1, HOME), 1, sibling), rows((HOME, 0, 0), (HOME, 1, 0), 3, sibling)]
            )
            self.all_tiles = [tiles((r, 0, 0), (r, 1, 0), 4, sibling) for r in range(4)]

        def first(self):
            start(self.own_tiles)
            start(self.own_a)
            for r in (1, 2, 0):
                self.to_b[r][0].start()
            self.across[HOME][0].start()

        def second(self):
            arrive(self.own_tiles)
            self.all_tiles[HOME].start()
            start(self.b_tiles)
            self.own_a[1].wait_recv()
            self.own_a[2].wait_recv()
            for r in (1, 2, 0):
                self.to_b[r][1].start()
            self.own_a[0].wait_recv()
            for r in (1, 2, 0):
                self.to_b[r][2].start()
            self.across[HOME][1].start()

        def share_tiles(self):
            arrive(self.b_tiles)
            start(self.all_tiles[:HOME])

        def share(self, r):
            arrive(self.to_b[BACK[r]])
            start(self.across[r])

    near, far = Gather(q, packed), Gather(far_q, far_packed)
    near.first()
    exchange = [
        send(q.at[own], far_q.at[own], opposite),
        send(packed.at[own_tile], far_packed.at[own_tile], opposite),
    ]

    def unpack(packed, weights, held, blocks, lo, hi):
        ids, halves = unpack_rows(packed, lo, hi)
        rows, count = pl.ds(lo * ROWS, (hi - lo) * ROWS), (hi - lo) * ROWS
        sub = lax.broadcasted_iota(jnp.int32, (8, count), 0)
        weights[:, rows] = jnp.broadcast_to(halves, (8, count))
        label = ids - l * (4 * NZ * LAB)
        mine = (label >= 0) & (label < 4 * NZ * LAB) & (((label >> 8) & 3) == yc)
        word = jnp.where(mine, (label >> 10) * 8 + (label & 7), -1)
        bit = lax.shift_left(jnp.int32(1), (label >> 3) & 31)
        for n, j in enumerate(blocks):
            words = jnp.zeros((8, count), jnp.int32)
            for s in range(POS):
                hit = word[s : s + 1] == plane_at(AWAY[j]) * 8 + sub
                words = words | jnp.where(hit, bit[s : s + 1], 0)
            held[n, :, rows] = words

    def block(j, count):
        return pl.ds(j * LAB, count * LAB)

    def gradient(j, count, rows, held, scale):
        logits = lax.dot_general(
            w[block(j, count), :], rows, (((1,), (1,)), ((), ())), preferred_element_type=F32
        )
        parts = []
        for n in range(count):
            for k in range(LAB // 8):
                mask = jnp.int32(1 << k if k < 31 else -(1 << 31))
                target = jnp.where((held[n] & mask) != 0, -1.0, 1.0)
                at = n * LAB + 8 * k
                parts.append(scale * (jnp.tanh(0.5 * logits[at : at + 8]) + target))
        return jnp.concatenate(parts, axis=0).astype(BF16)

    def forward(j, count, rows, out, first=False):
        held = [bits[j + n, :, rows] for n in range(count)]
        out[...] = gradient(j, count, q[rows, :], held, half_weight[:, rows])
        part = lax.dot_general(
            out[...], w[block(j, count), :], (((0,), (0,)), ((), ())), preferred_element_type=F32
        )
        if first:
            qg[rows, :] = part
        else:
            qg[rows, :] += part

    def backward(j, count, rows, grads, first=False):
        part = jnp.dot(grads[...], q[rows, :], preferred_element_type=F32)
        if first:
            wg[block(j, count), :] = part
        else:
            wg[block(j, count), :] += part

    def far_backward(j, count):
        out = far_g.at[pl.ds(0, count * LAB)]
        held = [far_bits[j - 2 + n] for n in range(count)]
        out[...] = gradient(j, count, far_q[...], held, far_weight[...])
        wg[block(j, count), :] += jnp.dot(out[...], far_q[...], preferred_element_type=F32)

    def chunk(r):
        return pl.ds(r * CHUNK, CHUNK)

    def grads_of(count, rows):
        return g.at[pl.ds(0, count * LAB), rows]

    others, everyone = pl.ds(0, HOME * CHUNK), pl.ds(0, PLANE)
    crossed, along_b, along_a = [None] * 4, [], []

    def cross(r):
        sib_s[r] = qg[place(r, 1, 0, 4), :].astype(BF16)
        crossed[r] = send(sib_s.at[r], sib_r.at[r], sibling)

    def go_b(r):
        crossed[r].wait_recv()
        rows = place(r, 0, 0, 4)
        total = qg[rows, :] + sib_r[r].astype(F32)
        if r == HOME:
            qg[rows, :] = total
        else:
            one_s[r] = total.astype(BF16)
            along_b.append(send(one_s.at[r], one_r.at[r], to_b[r]))

    near.second()
    arrive(exchange)
    far.first()
    near.all_tiles[HOME].wait_recv()
    unpack(packed, half_weight, bits, range(8), 24, 32)
    for load in loads[3:]:
        load.wait()
    arrive(near.across[HOME])
    forward(0, 4, chunk(HOME), grads_of(4, chunk(HOME)), first=True)
    backward(0, 4, chunk(HOME), grads_of(4, chunk(HOME)), first=True)
    near.share_tiles()
    near.share(1)
    near.share(2)
    arrive(near.all_tiles[:HOME])
    unpack(packed, half_weight, bits, range(8), 0, 24)
    for r in (1, 2, 0):
        if r == 2:
            near.share(0)
            far.second()
        arrive(near.across[r])
        grads = grads_of(2, chunk(r))
        forward(0, 2, chunk(r), grads, first=True)
        backward(0, 2, chunk(r), grads)

    passes = [[prepare(zs.at[t, m], zr.at[t, m], to_z[t]) for m in range(4)] for t in range(2)]

    def pass_on(m, way):
        total = wg[pl.ds((2 * (m // 2) + way) * LAB + m % 2 * HALF, HALF), :]
        if m >= 2:
            passes[way][m - 2].wait_recv()
            total = total + zr[way, m - 2].astype(F32)
        zs[way, m] = total.astype(BF16)
        passes[way][m].start()

    for m in range(2):
        pass_on(m, 0)
        pass_on(m, 1)

    for j in (2, 3):
        forward(j, 1, others, grads_of(1, others))
        backward(j, 1, others, grads_of(1, others))

    for r in range(3):
        forward(4, 4, chunk(r), grads_of(4, chunk(r)))
        cross(r)
        if r > 0:
            go_b(r - 1)
        if r == 0:
            far.share_tiles()
        if r == 1:
            for k in (1, 2, 0):
                far.share(k)
    arrive(far.all_tiles)
    unpack(far_packed, far_weight, far_bits, (2, 3, 4), 0, 32)
    for r in range(4):
        arrive(far.across[r])
    for way in range(2):
        far_backward(2 + way, 1)
        pass_on(2, way)
        pass_on(3, way)
        if way == 0:
            go_b(2)
    forward(4, 4, chunk(HOME), grads_of(4, chunk(HOME)))
    cross(HOME)
    backward(4, 1, everyone, grads_of(1, everyone), first=True)
    go_b(HOME)

    for copy in copies[:GATHERED]:
        copy.wait_send()
    arrive(along_b)
    for i in range(4):
        part = pl.ds(i * ROWS, ROWS)
        total = qg[place(HOME, 0, i), :]
        for r in range(3):
            total = total + one_r[r, part, :].astype(F32)
        if i == HOME:
            query_grad[...] = total
        else:
            two_s[i] = total.astype(BF16)
            along_a.append(send(two_s.at[i], two_r.at[i], to_a[i]))
    far_backward(4, 1)
    stores = []
    for m in (2, 3):
        half = pl.ds((m - 2) * HALF, HALF)
        total = wg[pl.ds(4 * LAB + (m - 2) * HALF, HALF), :]
        for way in range(2):
            passes[way][m].wait_recv()
            total = total + zr[way, m].astype(F32)
        weight_grad[half, :] = total
        stores.append(pltpu.make_async_copy(weight_grad.at[half], weight_out.at[half], out_sem.at[m - 2]))
        stores[-1].start()
    for i in range(3):
        along_a[i].wait_recv()
        query_grad[...] += two_r[i].astype(F32)
    stores.append(pltpu.make_async_copy(query_grad, query_out, out_sem.at[2]))
    stores[-1].start()

    for copy in copies[GATHERED:]:
        copy.wait_send()
    for store in stores:
        store.wait()


GATHERED = 2 * 27 + 2
COPIES = GATHERED + 8 + 4 + 3 + 3


def hand_over(query_in, weight_in, query_out, weight_out):
    query_out[...] = query_in[...]
    weight_out[...] = weight_in[...]


def on_device(queries, positives, row_weight, label_weight):
    vmem = pl.BlockSpec(memory_space=pltpu.VMEM)
    hbm = pl.BlockSpec(memory_space=pl.ANY)
    outs = (jax.ShapeDtypeStruct((ROWS, D), F32), jax.ShapeDtypeStruct((LAB, D), F32))
    grads = pl.pallas_call(
        kernel,
        out_shape=outs,
        in_specs=[hbm, hbm, hbm, hbm],
        out_specs=(hbm, hbm),
        scratch_shapes=[
            pltpu.VMEM((ROWS, D), F32),
            pltpu.VMEM((LAB, D), F32),
            pltpu.SemaphoreType.DMA((3,)),
            pltpu.VMEM((PLANE, D), BF16),
            pltpu.VMEM((PLANE, D), BF16),
            pltpu.VMEM((32, 16, 128), BF16),
            pltpu.VMEM((32, 16, 128), BF16),
            pltpu.VMEM((NZ * LAB, D), BF16),
            pltpu.VMEM((PLANE, D), F32),
            pltpu.VMEM((5 * LAB, D), F32),
            pltpu.VMEM((4 * LAB, PLANE), BF16),
            pltpu.VMEM((LAB, PLANE), BF16),
            pltpu.VMEM((NZ, 8, PLANE), jnp.int32),
            pltpu.VMEM((8, PLANE), F32),
            pltpu.VMEM((3, 8, PLANE), jnp.int32),
            pltpu.VMEM((8, PLANE), F32),
            pltpu.VMEM((POS, ROWS), jnp.int32),
            pltpu.VMEM((1, ROWS), F32),
            pltpu.VMEM((2, 4, HALF, D), BF16),
            pltpu.VMEM((2, 4, HALF, D), BF16),
            pltpu.VMEM((4, 4 * ROWS, D), BF16),
            pltpu.VMEM((4, 4 * ROWS, D), BF16),
            pltpu.VMEM((3, 4 * ROWS, D), BF16),
            pltpu.VMEM((3, 4 * ROWS, D), BF16),
            pltpu.VMEM((3, ROWS, D), BF16),
            pltpu.VMEM((3, ROWS, D), BF16),
            pltpu.SemaphoreType.DMA((NZ + 3,)),
            pltpu.SemaphoreType.DMA((COPIES,)),
            pltpu.SemaphoreType.DMA((COPIES,)),
        ],
        compiler_params=pltpu.CompilerParams(
            collective_id=0, has_side_effects=True, vmem_limit_bytes=56 * 2**20
        ),
        cost_estimate=pl.CostEstimate(
            flops=6 * PLANE * NZ * LAB * D, bytes_accessed=NZ * LAB * D * 2, transcendentals=0
        ),
    )(queries, positives.T, row_weight[None, :], label_weight)
    return pl.pallas_call(
        hand_over,
        out_shape=outs,
        in_specs=[vmem, vmem],
        out_specs=(vmem, vmem),
        compiler_params=pltpu.CompilerParams(vmem_limit_bytes=56 * 2**20),
    )(*grads)


def solution(mesh):
    placed = (
        P(("label", "dp"), None),
        P(("label", "dp"), None),
        P(("label", "dp")),
        P("label", None),
    )
    return jax.shard_map(
        on_device,
        mesh=mesh,
        in_specs=placed,
        out_specs=(P(("label", "dp"), None), P(("label", "dp"), None)),
        check_vma=False,
    )
```
